32 devices in a mesh: dp: 16 (over z, y, core), tensor: 2 (over x).
Axes of the slice: x: 2, y: 2, z: 4, core: 2. Of those that a mesh axis runs over, the one named last changes fastest.
Arguments:
- cotangent: bfloat16 [16384, 3072], P(('dp', 'tensor')), may hold values from -6 to 6
- context: bfloat16 [16384, 3072], P('dp', 'tensor'), may hold values from -6 to 6
- master: float32 [3072, 3072], P('dp', 'tensor'), may hold values from -0.109375 to 0.109375
- first_moment: float32 [3072, 3072], P('dp', 'tensor'), may hold values from -0.046875 to 0.046875
- second_moment: float32 [3072, 3072], P('dp', 'tensor'), as said below
Outputs:
- d_context: bfloat16 [16384, 3072], P('dp', 'tensor')
- new_master: float32 [3072, 3072], P('dp', 'tensor')
- new_first: float32 [3072, 3072], P('dp', 'tensor')
- new_second: float32 [3072, 3072], P('dp', 'tensor')
- new_weights: bfloat16 [3072, 3072], P(None, 'tensor')
The draws below stay inside these ranges and needn't reach their ends.
Inputs may be any that keep to these rules, and one draw needn't show every extreme that they name: second_moment is positive.
All inputs are finite; a program needn't handle non-finite values.
Results may differ from the reference program's by a relative error of at most 0.0049.
Values may be sent and summed in bfloat16 or wider, within the bound.
A program may use at most 128 MiB of HBM per device.

```python
import jax
import jax.numpy as jnp
from jax import lax

HEADS = 24
HD = 128
DW = 3072
STEP = 10
TOKENS = 16384
HHD = 3072


def draw_second_moment(key, part):
    unit = jax.random.uniform(key, (DW, HEADS * HD), jnp.float32)
    return jnp.exp(jnp.log(0.1) + unit * jnp.log(10.0)) / TOKENS


def steps_of(rng, shape, split, least, largest):
    loudness = 1.0
    for axis_at, shards_of in split:
        steps = jax.random.uniform(jax.random.fold_in(jax.random.fold_in(rng, 6), axis_at), (shards_of,), jnp.float32, least / len(split), largest / len(split))
        loudness = loudness * jnp.repeat(jnp.exp(steps), shape[axis_at] // shards_of).reshape((-1,) + (1,) * (len(shape) - 1 - axis_at))
    return loudness


def gaussian(own_key, extent, scale, limit, shards=(), dtype=jnp.bfloat16):
    entries = jax.random.normal(own_key, extent, jnp.float32) * scale
    if len(shards) > 0:
        entries = steps_of(own_key, extent, shards, -0.22, 0.18) * entries
    return jnp.clip(entries, min=-limit, max=limit).astype(dtype)


def setup_inputs(seed: int = 0) -> dict:
    seeds = jax.random.split(jax.random.key(seed), 6)
    return {
        "cotangent": gaussian(seeds[0], (TOKENS, DW), 1.0, 6.0, ((0, 32),)),
        "context": gaussian(seeds[1], (TOKENS, HHD), 1.0, 6.0, ((0, 16), (1, 2))),
        "master": gaussian(seeds[2], (DW, HHD), HHD ** -0.5, 0.109375, ((0, 16), (1, 2)), jnp.float32),
        "first_moment": gaussian(seeds[3], (DW, HHD), TOKENS ** -0.5, 0.046875, ((0, 16), (1, 2)), jnp.float32),
        "second_moment": draw_second_moment(jax.random.fold_in(seeds[5], 71), 0),
    }


def reference(cotangent, context, master, first_moment, second_moment):
    weights = master.astype(jnp.bfloat16)
    d_context = jnp.dot(cotangent, weights, preferred_element_type=jnp.float32).astype(jnp.bfloat16)
    total = lax.dot_general(cotangent, context, (((0,), (0,)), ((), ())), preferred_element_type=jnp.float32)
    grad = total / jnp.float32(TOKENS)
    new_first = 0.9 * first_moment + 0.1 * grad
    new_second = 0.95 * second_moment + 0.05 * grad * grad
    first_scale = 1.0 - 0.9 ** STEP
    second_scale = 1.0 - 0.95 ** STEP
    update = new_first / first_scale / (jnp.sqrt(new_second / second_scale) + 1e-08)
    new_master = master - 0.001 * update
    new_weights = new_master.astype(jnp.bfloat16)
    return (d_context, new_master, new_first, new_second, new_weights)
```

```python
import functools

import jax
import jax.numpy as jnp
from jax import lax
from jax.experimental import pallas as pl
from jax.experimental.pallas import tpu as pltpu
from jax.sharding import PartitionSpec as P

STEP = 10
F32 = jnp.float32
BF16 = jnp.bfloat16


def tile_of(extent, most):
    best = extent
    for size in range(128, most + 1, 128):
        if extent % size == 0:
            best = size
    return best if best <= most else extent


def kernel(
    A, B, T, tokens,
    cot, ctx_in, mas, mom, var,
    dctx, nmas, nmom, nvar, nw,
    ctx, cotg, wfull, own, s1, r1, qown, s2, r2, s3, r3, nown,
    loc_sem, cs_sem, cr_sem, ws_sem, wr_sem, ns_sem, nr_sem,
    s1_sem, r1_sem, s2_sem, r2_sem, s3_sem, r3_sem,
):
    G = A * B
    R, N = mas.shape
    tk = ctx.shape[1]
    nt = tile_of(N, 512)
    me = lax.axis_index("dp")
    t = lax.axis_index("tensor")
    chip = me // 2
    c = me % 2
    a = chip // B
    b = chip % B

    def flat(a_, b_, c_):
        return (a_ * B + b_) * 2 + c_

    a_of = [lax.rem(a + i, A) for i in range(A)]
    b_of = [lax.rem(b + i, B) for i in range(B)]
    t_of = [lax.rem(t + i, T) for i in range(T)]
    sib = flat(a, b, 1 - c)
    sends = []

    def send(src, dst, ssem, rsem, where):
        copy = pltpu.make_async_remote_copy(
            src_ref=src, dst_ref=dst, send_sem=ssem, recv_sem=rsem,
            device_id=where, device_id_type=pl.DeviceIdType.MESH,
        )
        copy.start()
        sends.append(copy)

    def arrived(dst, ssem, rsem):
        pltpu.make_async_remote_copy(
            src_ref=dst, dst_ref=dst, send_sem=ssem, recv_sem=rsem,
            device_id={"dp": sib}, device_id_type=pl.DeviceIdType.MESH,
        ).wait_recv()

    barrier = pltpu.get_barrier_semaphore()
    peers = [{"dp": flat(a_of[i], b, c)} for i in range(1, A)]
    peers += [{"dp": flat(a, b_of[i], c)} for i in range(1, B)]
    peers += [{"dp": sib}]
    peers += [{"tensor": t_of[i]} for i in range(1, T)]
    for where in peers:
        pl.semaphore_signal(barrier, inc=1, device_id=where, device_id_type=pl.DeviceIdType.MESH)
    pl.semaphore_wait(barrier, len(peers))

    order = [(ai, bi) for ai in [*range(1, A), 0] for bi in [*range(1, B), 0]]

    def group(k):
        ai, bi = order[k]
        return a_of[ai] * B + b_of[bi]

    def exchange(k):
        g = group(k)
        for i in range(1, T):
            send(cot.at[g], cotg.at[t, g], cs_sem.at[k, i - 1], cr_sem.at[k, i - 1], {"tensor": t_of[i]})

    ahead = 3
    for k in range(min(ahead, G)):
        exchange(k)
    ctx_copy = pltpu.make_async_copy(ctx_in, ctx, loc_sem.at[0])
    ctx_copy.start()
    cot_copy = pltpu.make_async_copy(cot, cotg.at[t], loc_sem.at[1])
    cot_copy.start()

    class Gather:
        def __init__(self, src, buf, ssem, rsem):
            self.src, self.buf, self.ssem, self.rsem, self.n = src, buf, ssem, rsem, 0

        def put(self, src, d, where):
            send(src, self.buf.at[d], self.ssem.at[self.n], self.rsem.at[d], {"dp": where})
            self.n += 1

        def first(self):
            for i in range(1, A):
                self.put(self.src, me, flat(a_of[i], b, c))
            for i in range(1, B):
                self.put(self.src, me, flat(a, b_of[i], c))
            self.put(self.src, me, sib)

        def wait(self, d):
            arrived(self.buf.at[d], self.ssem.at[0], self.rsem.at[d])

        def along_a(self, i):
            d = flat(a_of[A - i], b, c)
            self.wait(d)
            for j in range(1, B):
                self.put(self.buf.at[d], d, flat(a, b_of[j], c))
            self.put(self.buf.at[d], d, sib)

        def along_b(self, i):
            for j in range(1, B):
                d = flat(a_of[(A - i) % A], b_of[j], c)
                self.wait(d)
                self.put(self.buf.at[d], d, sib)

        def last(self):
            for i in range(A):
                for j in range(B):
                    self.wait(flat(a_of[i], b_of[j], 1 - c))

    wfull[me] = mas[...].astype(BF16)
    weights = Gather(wfull.at[me], wfull, ws_sem, wr_sem)
    weights.first()
    ctx_copy.wait()
    cot_copy.wait()

    def partial(g, core, store):
        def tile(n, carry):
            cols = pl.ds(pl.multiple_of(n * nt, nt), nt)
            total = jnp.dot(cotg[0, g, core], ctx[0, :, cols], preferred_element_type=F32)
            for i in range(1, T):
                total = total + jnp.dot(cotg[i, g, core], ctx[i, :, cols], preferred_element_type=F32)
            store(cols, total)
            return carry

        lax.fori_loop(0, N // nt, tile, 0)

    def stage2(k):
        ai, bi = order[k]
        arrived(r1.at[k], s1_sem.at[k], r1_sem.at[k])
        q = own[k % 2] + r1[k].astype(F32)
        if bi:
            j = ai * (B - 1) + bi - 1
            s2[j] = q.astype(BF16)
            send(s2.at[j], r2.at[j], s2_sem.at[j], r2_sem.at[j], {"dp": flat(a, b_of[bi], c)})
        else:
            qown[ai % 2] = q

    def stage3(ai):
        q = qown[ai % 2]
        for bi in range(1, B):
            j = ai * (B - 1) + bi - 1
            arrived(r2.at[j], s2_sem.at[j], r2_sem.at[j])
            q = q + r2[j].astype(F32)
        if ai:
            s3[ai - 1] = q.astype(BF16)
            send(s3.at[ai - 1], r3.at[ai - 1], s3_sem.at[ai - 1], r3_sem.at[ai - 1], {"dp": flat(a_of[ai], b, c)})
        return q

    forwarded = 0
    for k in range(G):
        g = group(k)
        for i in range(1, T):
            arrived(cotg.at[t_of[T - i], g], cs_sem.at[k, i - 1], cr_sem.at[k, i - 1])
        if k + ahead < G:
            exchange(k + ahead)

        def to_sibling(cols, total):
            s1[k, :, cols] = total.astype(BF16)

        def to_own(cols, total):
            own[k % 2, :, cols] = total

        partial(g, 1 - c, to_sibling)
        send(s1.at[k], r1.at[k], s1_sem.at[k], r1_sem.at[k], {"dp": sib})
        partial(g, c, to_own)
        if k:
            stage2(k - 1)
        if k % B == B - 1 and k // B >= 1:
            stage3(order[k - B][0])
        if (k + 1) * (A - 1) // G > forwarded:
            forwarded += 1
            weights.along_a(forwarded)
    stage2(G - 1)
    q = stage3(0)
    for i in range(1, A):
        arrived(r3.at[i - 1], s3_sem.at[i - 1], r3_sem.at[i - 1])
        q = q + r3[i - 1].astype(F32)

    grad = q / jnp.float32(tokens)
    new_first = 0.9 * mom[...] + 0.1 * grad
    new_second = 0.95 * var[...] + 0.05 * grad * grad
    update = new_first / (1.0 - 0.9**STEP) / (jnp.sqrt(new_second / (1.0 - 0.95**STEP)) + 1e-08)
    new_master = mas[...] - 0.001 * update
    nown[...] = new_master.astype(BF16)
    fresh = Gather(nown, nw, ns_sem, nr_sem)
    fresh.first()
    nmom[...] = new_first
    nvar[...] = new_second
    nmas[...] = new_master
    own_copy = pltpu.make_async_copy(nown, nw.at[me], loc_sem.at[0])
    own_copy.start()

    for i in range(A):
        weights.along_b(i)
    weights.last()

    mt = tile_of(tk, 256)

    def columns(n):
        cols = pl.ds(pl.multiple_of(n * nt, nt), nt)

        def tile(i, carry):
            rows = pl.ds(pl.multiple_of((i % (tk // mt)) * mt, mt), mt)
            left = cotg[i // (tk // mt), :, :, :, rows].reshape(G * 2 * R, mt)
            right = wfull[:, :, cols].reshape(G * 2 * R, nt)
            total = lax.dot_general(left, right, (((0,), (0,)), ((), ())), preferred_element_type=F32)
            dctx[pl.ds(pl.multiple_of(i * mt, mt), mt), cols] = total.astype(BF16)
            return carry

        lax.fori_loop(0, T * (tk // mt), tile, 0)

    steps = max(N // nt, A - 1)
    for i in range(steps):
        if i < N // nt:
            columns(i)
        if i < A - 1:
            fresh.along_a(i + 1)
    for i in range(A):
        fresh.along_b(i)
    fresh.last()
    own_copy.wait()
    for copy in sends:
        copy.wait_send()


def body(A, B, T, cotangent, context, master, first_moment, second_moment):
    R, N = master.shape
    G = A * B
    dp = G * 2
    tk = cotangent.shape[0]
    cot = cotangent.T.reshape(G, 2, R, tk)
    ctx = context.reshape(T, tk, N)
    dma = pltpu.SemaphoreType.DMA
    hbm = pl.BlockSpec(memory_space=pl.ANY)
    vmem = pl.BlockSpec(memory_space=pltpu.VMEM)
    state = jax.ShapeDtypeStruct((R, N), F32)
    gathers = A - 1 + A * (B - 1) + A * B
    dctx, nmas, nmom, nvar, nw = pl.pallas_call(
        functools.partial(kernel, A, B, T, tk * T * dp),
        out_shape=(
            jax.ShapeDtypeStruct((T * tk, N), BF16),
            state, state, state,
            jax.ShapeDtypeStruct((dp, R, N), BF16),
        ),
        in_specs=[hbm, hbm, vmem, vmem, vmem],
        out_specs=(vmem, vmem, vmem, vmem, hbm),
        scratch_shapes=[
            pltpu.VMEM((T, tk, N), BF16),
            pltpu.VMEM((T, G, 2, R, tk), BF16),
            pltpu.VMEM((dp, R, N), BF16),
            pltpu.VMEM((2, R, N), F32),
            pltpu.VMEM((G, R, N), BF16),
            pltpu.VMEM((G, R, N), BF16),
            pltpu.VMEM((2, R, N), F32),
            pltpu.VMEM((A * (B - 1), R, N), BF16),
            pltpu.VMEM((A * (B - 1), R, N), BF16),
            pltpu.VMEM((A - 1, R, N), BF16),
            pltpu.VMEM((A - 1, R, N), BF16),
            pltpu.VMEM((R, N), BF16),
            dma((2,)),
            dma((G, T - 1)), dma((G, T - 1)),
            dma((gathers,)), dma((dp,)),
            dma((gathers,)), dma((dp,)),
            dma((G,)), dma((G,)),
            dma((A * (B - 1),)), dma((A * (B - 1),)),
            dma((A - 1,)), dma((A - 1,)),
        ],
        compiler_params=pltpu.CompilerParams(
            collective_id=0, has_side_effects=True, vmem_limit_bytes=60 * 1024 * 1024
        ),
    )(cot, ctx, master, first_moment, second_moment)
    return dctx, nmas, nmom, nvar, nw.reshape(dp * R, N)


def solution(mesh):
    dp, T = mesh.shape["dp"], mesh.shape["tensor"]
    A = 4
    B = dp // (2 * A)
    in_specs = (
        P(("dp", "tensor"), None),
        P("dp", "tensor"),
        P("dp", "tensor"),
        P("dp", "tensor"),
        P("dp", "tensor"),
    )
    out_specs = (
        P("dp", "tensor"),
        P("dp", "tensor"),
        P("dp", "tensor"),
        P("dp", "tensor"),
        P(None, "tensor"),
    )
    return jax.shard_map(
        functools.partial(body, A, B, T),
        mesh=mesh, in_specs=in_specs, out_specs=out_specs, check_vma=False,
    )
```

```python
import functools

import jax
import jax.numpy as jnp
from jax import lax
from jax.experimental import pallas as pl
from jax.experimental.pallas import tpu as pltpu
from jax.sharding import PartitionSpec as P

STEP = 10
F32 = jnp.float32
BF16 = jnp.bfloat16
PARTS = 8


def tile_of(extent, most):
    best = extent
    for size in range(128, most + 1, 128):
        if extent % size == 0:
            best = size
    return best if best <= most else extent


def kernel(
    A, B, T, tokens,
    cot, ctx_in, mas, mom, var,
    dctx, nmas, nmom, nvar, nw_out,
    ctx, cotg, wfull, own, s1, r1, qown, s2, r2, s3, r3, nown, nw,
    loc_sem, out_sem, cs_sem, cr_sem, ws_sem, wr_sem, ns_sem, nr_sem,
    s1_sem, r1_sem, s2_sem, r2_sem, s3_sem, r3_sem,
):
    G = A * B
    R, N = mas.shape
    tk = ctx.shape[1]
    nt = tile_of(N, 512)
    me = lax.axis_index("dp")
    t = lax.axis_index("tensor")
    chip = me // 2
    c = me % 2
    a = chip // B
    b = chip % B

    def flat(a_, b_, c_):
        return (a_ * B + b_) * 2 + c_

    a_of = [lax.rem(a + i, A) for i in range(A)]
    b_of = [lax.rem(b + i, B) for i in range(B)]
    t_of = [lax.rem(t + i, T) for i in range(T)]
    sib = flat(a, b, 1 - c)
    sends = []

    held = []
    H = 2 if R % 32 == 0 else 1

    def remote(src, dst, ssem, rsem, where):
        return pltpu.make_async_remote_copy(
            src_ref=src, dst_ref=dst, send_sem=ssem, recv_sem=rsem,
            device_id=where, device_id_type=pl.DeviceIdType.MESH,
        )

    def send(*args):
        copy = remote(*args)
        copy.start()
        sends.append(copy)

    def arrived(dst, ssem, rsem):
        pltpu.make_async_remote_copy(
            src_ref=dst, dst_ref=dst, send_sem=ssem, recv_sem=rsem,
            device_id={"dp": sib}, device_id_type=pl.DeviceIdType.MESH,
        ).wait_recv()

    barrier = pltpu.get_barrier_semaphore()
    peers = [{"dp": flat(a_of[i], b, c)} for i in range(1, A)]
    peers += [{"dp": flat(a, b_of[i], c)} for i in range(1, B)]
    peers += [{"dp": sib}]
    peers += [{"tensor": t_of[i]} for i in range(1, T)]
    for where in peers:
        pl.semaphore_signal(barrier, inc=1, device_id=where, device_id_type=pl.DeviceIdType.MESH)
    pl.semaphore_wait(barrier, len(peers))

    far = sorted(range(1, A), key=lambda i: abs(2 * i - A))
    order = [(ai, bi) for ai in [*far, 0] for bi in [*range(1, B), 0]]

    def group(k):
        ai, bi = order[k]
        return a_of[ai] * B + b_of[bi]

    def exchange(k):
        g = group(k)
        for i in range(1, T):
            send(cot.at[g], cotg.at[t, g], cs_sem.at[k, i - 1], cr_sem.at[k, i - 1], {"tensor": t_of[i]})

    ahead = 3
    for k in range(min(ahead, G)):
        exchange(k)
    ctx_copy = pltpu.make_async_copy(ctx_in, ctx, loc_sem.at[0])
    ctx_copy.start()
    cot_copy = pltpu.make_async_copy(cot, cotg.at[t], loc_sem.at[1])
    cot_copy.start()

    class Gather:
        def __init__(self, src, buf, ssem, rsem, across_first):
            self.src, self.buf, self.ssem, self.rsem, self.n = src, buf, ssem, rsem, 0
            self.across_first = across_first

        def rows(self, ref, h):
            return ref.at[pl.ds(h * (R // H), R // H)]

        def put(self, src, d, h, where, cond=None):
            args = (
                self.rows(src, h), self.rows(self.buf.at[d], h),
                self.ssem.at[self.n], self.rsem.at[d * H + h], {"dp": where},
            )
            self.n += 1
            if cond is None:
                send(*args)
            else:
                held.append((cond, args))

                @pl.when(cond)
                def _():
                    remote(*args).start()

        def line(self, src, d, h, up, cond=True):
            if up:
                self.put(src, d, h, flat(lax.rem(a + 1, A), b, c), jnp.logical_and(cond, a < A - 1))
            else:
                self.put(src, d, h, flat(lax.rem(a + A - 1, A), b, c), jnp.logical_and(cond, a > 0))

        def first(self, h):
            self.line(self.src, me, h, True)
            self.line(self.src, me, h, False)
            for i in range(1, B):
                self.put(self.src, me, h, flat(a, b_of[i], c))
            self.put(self.src, me, h, sib)

        def wait(self, d, h):
            arrived(self.rows(self.buf.at[d], h), self.ssem.at[0], self.rsem.at[d * H + h])

        def across(self, h):
            for j in range(1, B) if self.across_first[h] else ():
                d = flat(a, b_of[j], c)
                self.wait(d, h)
                self.line(self.buf.at[d], d, h, True)
                self.line(self.buf.at[d], d, h, False)
                self.put(self.buf.at[d], d, h, sib)

        def hop(self, s, h):
            for j in range(B) if self.across_first[h] else (0,):
                for up in (True, False):
                    cond = a >= s if up else a + s < A
                    d = flat(lax.rem(a + (A - s if up else s), A), b_of[j], c)

                    @pl.when(cond)
                    def _():
                        self.wait(d, h)

                    self.line(self.buf.at[d], d, h, up, cond)
                    for i in range(1, B) if not self.across_first[h] else ():
                        self.put(self.buf.at[d], d, h, flat(a, b_of[i], c), cond)
                    self.put(self.buf.at[d], d, h, sib, cond)

        def rest(self, h, s):
            if self.across_first[h]:
                return
            for j in range(1, B):
                d = flat(a_of[s], b_of[j], c)
                self.wait(d, h)
                self.put(self.buf.at[d], d, h, sib)

        def last(self, then=lambda d: None):
            for i in range(A):
                for j in range(B):
                    d = flat(a_of[i], b_of[j], 1 - c)
                    for h in range(H):
                        self.wait(d, h)
                    then(d)

    wfull[me] = mas[...].astype(BF16)
    weights = Gather(wfull.at[me], wfull, ws_sem, wr_sem, [h == 1 for h in range(H)])
    for h in range(H):
        weights.first(h)
    ctx_copy.wait()
    cot_copy.wait()

    def partial(g, core, store):
        def tile(n, carry):
            cols = pl.ds(pl.multiple_of(n * nt, nt), nt)
            total = jnp.dot(cotg[0, g, core], ctx[0, :, cols], preferred_element_type=F32)
            for i in range(1, T):
                total = total + jnp.dot(cotg[i, g, core], ctx[i, :, cols], preferred_element_type=F32)
            store(cols, total)
            return carry

        lax.fori_loop(0, N // nt, tile, 0)

    def stage2(k):
        ai, bi = order[k]
        arrived(r1.at[k], s1_sem.at[k], r1_sem.at[k])
        q = own[k % 2] + r1[k].astype(F32)
        if bi:
            j = ai * (B - 1) + bi - 1
            s2[j] = q.astype(BF16)
            send(s2.at[j], r2.at[j], s2_sem.at[j], r2_sem.at[j], {"dp": flat(a, b_of[bi], c)})
        else:
            qown[ai % 2] = q

    def stage3(ai):
        q = qown[ai % 2]
        for bi in range(1, B):
            j = ai * (B - 1) + bi - 1
            arrived(r2.at[j], s2_sem.at[j], r2_sem.at[j])
            q = q + r2[j].astype(F32)
        if ai:
            s3[ai - 1] = q.astype(BF16)
            send(s3.at[ai - 1], r3.at[ai - 1], s3_sem.at[ai - 1], r3_sem.at[ai - 1], {"dp": flat(a_of[ai], b, c)})
        return q

    forwarded = 0
    for k in range(G):
        g = group(k)
        for i in range(1, T):
            arrived(cotg.at[t_of[T - i], g], cs_sem.at[k, i - 1], cr_sem.at[k, i - 1])
        if k + ahead < G:
            exchange(k + ahead)

        def to_sibling(cols, total):
            s1[k, :, cols] = total.astype(BF16)

        def to_own(cols, total):
            own[k % 2, :, cols] = total

        partial(g, 1 - c, to_sibling)
        send(s1.at[k], r1.at[k], s1_sem.at[k], r1_sem.at[k], {"dp": sib})
        partial(g, c, to_own)
        if k:
            stage2(k - 1)
        if k and k % B == 0:
            stage3(order[k - 1][0])
        if k == 1 or G == 1:
            for h in range(H):
                weights.across(h)
        if k > 1 and (k - 1) * (A - 1) // (G - 2) > forwarded:
            forwarded += 1
            for h in range(H):
                weights.hop(forwarded, h)
    stage2(G - 1)
    q = stage3(0)
    for i in range(1, A):
        arrived(r3.at[i - 1], s3_sem.at[i - 1], r3_sem.at[i - 1])
        q = q + r3[i - 1].astype(F32)

    fresh = Gather(nown, nw, ns_sem, nr_sem, [False] * H)
    for h in range(H):
        rows = pl.ds(h * (R // H), R // H)
        grad = q[h * (R // H) : (h + 1) * (R // H)] / jnp.float32(tokens)
        new_first = 0.9 * mom[rows] + 0.1 * grad
        new_second = 0.95 * var[rows] + 0.05 * grad * grad
        update = new_first / (1.0 - 0.9**STEP) / (jnp.sqrt(new_second / (1.0 - 0.95**STEP)) + 1e-08)
        new_master = mas[rows] - 0.001 * update
        nown[rows] = new_master.astype(BF16)
        fresh.first(h)
        nmom[rows] = new_first
        nvar[rows] = new_second
        nmas[rows] = new_master
    stores = []

    def store(d, src=None):
        src = nw.at[d] if src is None else src
        stores.append(pltpu.make_async_copy(src, nw_out.at[d], out_sem.at[len(stores)]))
        stores[-1].start()

    store(me, nown)

    for i in range(A):
        for h in range(H):
            weights.rest(h, i)
    for h in range(H):
        fresh.hop(1, h)
    weights.last()

    mt = tile_of(tk, 256)

    def columns(n):
        cols = pl.ds(pl.multiple_of(n * nt, nt), nt)

        def tile(i, carry):
            rows = pl.ds(pl.multiple_of((i % (tk // mt)) * mt, mt), mt)
            left = cotg[i // (tk // mt), :, :, :, rows].reshape(G * 2 * R, mt)
            right = wfull[:, :, cols].reshape(G * 2 * R, nt)
            total = lax.dot_general(left, right, (((0,), (0,)), ((), ())), preferred_element_type=F32)
            dctx[pl.ds(pl.multiple_of(i * mt, mt), mt), cols] = total.astype(BF16)
            return carry

        lax.fori_loop(0, T * (tk // mt), tile, 0)

    for i in range(max(N // nt, A - 2)):
        if i < N // nt:
            columns(i)
        if i < A - 2:
            for h in range(H):
                fresh.hop(i + 2, h)
    for i in range(A):
        for h in range(H):
            fresh.rest(h, i)
    for i in range(A):
        for j in range(B):
            if i or j:
                store(flat(a_of[i], b_of[j], c))
    fresh.last(store)
    for copy in stores:
        copy.wait()
    for copy in sends:
        copy.wait_send()
    for cond, args in held:

        @pl.when(cond)
        def _():
            remote(*args).wait_send()


def settle(*refs):
    n = (len(refs) - 2) // 3
    loads, stores = [], []
    for i in range(n):
        src, dst, held = refs[i], refs[n + i], refs[2 * n + i]
        size = src.shape[0] // PARTS
        parts = PARTS if size % 16 == 0 and size * PARTS == src.shape[0] and size > 64 else 1
        size = src.shape[0] // parts
        for j in range(parts):
            rows = pl.ds(j * size, size)
            loads.append(pltpu.make_async_copy(src.at[rows], held.at[rows], refs[-2].at[i, j]))
            stores.append(pltpu.make_async_copy(held.at[rows], dst.at[rows], refs[-1].at[i, j]))
    for load in loads:
        load.start()
    for load, store in zip(loads, stores):
        load.wait()
        store.start()
    for store in stores:
        store.wait()


def body(A, B, T, cotangent, context, master, first_moment, second_moment):
    R, N = master.shape
    G = A * B
    dp = G * 2
    tk = cotangent.shape[0]
    cot = cotangent.T.reshape(G, 2, R, tk)
    ctx = context.reshape(T, tk, N)
    dma = pltpu.SemaphoreType.DMA
    hbm = pl.BlockSpec(memory_space=pl.ANY)
    vmem = pl.BlockSpec(memory_space=pltpu.VMEM)
    state = jax.ShapeDtypeStruct((R, N), F32)
    gathers = 16 * A * B + 16
    dctx, nmas, nmom, nvar, nw = pl.pallas_call(
        functools.partial(kernel, A, B, T, tk * T * dp),
        out_shape=(
            jax.ShapeDtypeStruct((T * tk, N), BF16),
            state, state, state,
            jax.ShapeDtypeStruct((dp, R, N), BF16),
        ),
        in_specs=[hbm, hbm, vmem, vmem, vmem],
        out_specs=(vmem, vmem, vmem, vmem, hbm),
        scratch_shapes=[
            pltpu.VMEM((T, tk, N), BF16),
            pltpu.VMEM((T, G, 2, R, tk), BF16),
            pltpu.VMEM((dp, R, N), BF16),
            pltpu.VMEM((2, R, N), F32),
            pltpu.VMEM((G, R, N), BF16),
            pltpu.VMEM((G, R, N), BF16),
            pltpu.VMEM((2, R, N), F32),
            pltpu.VMEM((A * (B - 1), R, N), BF16),
            pltpu.VMEM((A * (B - 1), R, N), BF16),
            pltpu.VMEM((A - 1, R, N), BF16),
            pltpu.VMEM((A - 1, R, N), BF16),
            pltpu.VMEM((R, N), BF16),
            pltpu.VMEM((dp, R, N), BF16),
            dma((2,)), dma((dp,)),
            dma((G, T - 1)), dma((G, T - 1)),
            dma((gathers,)), dma((2 * dp,)),
            dma((gathers,)), dma((2 * dp,)),
            dma((G,)), dma((G,)),
            dma((A * (B - 1),)), dma((A * (B - 1),)),
            dma((A - 1,)), dma((A - 1,)),
        ],
        compiler_params=pltpu.CompilerParams(
            collective_id=0, has_side_effects=True, vmem_limit_bytes=63 * 1024 * 1024
        ),
    )(cot, ctx, master, first_moment, second_moment)
    results = (dctx, nmas, nmom, nvar, nw.reshape(dp * R, N))
    return pl.pallas_call(
        settle,
        out_shape=tuple(jax.ShapeDtypeStruct(x.shape, x.dtype) for x in results),
        in_specs=[hbm] * len(results),
        out_specs=(hbm,) * len(results),
        scratch_shapes=[pltpu.VMEM(x.shape, x.dtype) for x in results]
        + [dma((len(results), PARTS)), dma((len(results), PARTS))],
        compiler_params=pltpu.CompilerParams(vmem_limit_bytes=40 * 1024 * 1024),
    )(*results)


def solution(mesh):
    dp, T = mesh.shape["dp"], mesh.shape["tensor"]
    A = 4
    B = dp // (2 * A)
    in_specs = (
        P(("dp", "tensor"), None),
        P("dp", "tensor"),
        P("dp", "tensor"),
        P("dp", "tensor"),
        P("dp", "tensor"),
    )
    out_specs = (
        P("dp", "tensor"),
        P("dp", "tensor"),
        P("dp", "tensor"),
        P("dp", "tensor"),
        P(None, "tensor"),
    )
    return jax.shard_map(
        functools.partial(body, A, B, T),
        mesh=mesh, in_specs=in_specs, out_specs=out_specs, check_vma=False,
    )
```
